128 devices in a mesh: dir: 8 (over z, y_lo), bl: 16 (over x, y_hi, core).
Axes of the slice: x: 4, y: 4 (y_hi: 2, y_lo: 2; y = y_hi * 2 + y_lo), z: 4, core: 2. Of those that a mesh axis runs over, the one named last changes fastest.
Arguments:
- observed: float32 [32, 2, 61440], P('dir', None, 'bl'), may hold values from -6 to 6
- baseline_uvw_rows: float32 [3, 131072], P(None, 'bl'), may hold values from -600 to 600
- frequencies: float32 [32], replicated, may hold values from 0.8 to 1.2
- source_offset: float32 [2, 256], replicated, may hold values from -0.05 to 0.05
- source_flux: float32 [32, 256], replicated, may hold values from 0.02 to 0.3
- source_group: int32 [256], replicated, may hold values from 0 to 7, as said below
- direction_gain: float32 [8, 32, 2, 512], P('dir'), may hold values from -4.2 to 4.2
- station_first: int32 [8192], replicated, may hold values from 0 to 511
- station_second: int32 [8192], replicated, may hold values from 0 to 511
- average_exponent: int32 [8192], replicated, may hold values from 0 to 4, as said below
- owner_plan: int32 [16, 16], replicated, may hold values from 0 to 15, as said below
Outputs:
- residual: float32 [32, 2, 61440], P('dir', None, 'bl')
The draws below stay inside these ranges and needn't reach their ends.
Inputs may be any that keep to these rules, and one draw needn't show every extreme that they name: `source_group`: each of the 8 groups is named by exactly 32 sources. `average_exponent`: summed over the blocks that owner_plan gives one owner, the averaged rows are at most 3840, and some owner has exactly 3840. Each row of owner_plan names every owner exactly once.
All inputs are finite; a program needn't handle non-finite values.
Results may differ from the reference program's by a relative error of at most 0.0003.
Values sent between devices are 32-bit elements; how exact they have to be, the bound alone decides.
No kernel may reach another device: no remote copies, remote signals or barrier semaphores. Data moves between devices by JAX's collectives and lax.ppermute only.
A program may use at most 64 MiB of HBM per device.

```python
import math
import jax
import jax.numpy as jnp
from jax import lax

F = 32
TIME_SAMPLES = 16
STATION_COUNT = 512
SRC_GRP = 32
BL_DEV = 512
GROUPS = 8
SOURCES = 256
BLOCK = 32
BASELINE_COUNT = 8192
CAP_DEV = 3840
BDA_ROWS = 61440
N_DIR = 8
N_BL = 16


def shuffled(row_key):
    return jax.random.permutation(row_key, N_BL)


def plan_and_exponents(key):
    pick_key = jax.random.fold_in(key, 101)
    peak_key = jax.random.fold_in(key, 202)
    order_key = jax.random.fold_in(key, 303)
    jitter_key = jax.random.fold_in(key, 404)
    heavy_owner = jax.random.randint(pick_key, (), 0, N_BL)
    peak_block = jax.random.randint(peak_key, (N_BL,), 0, N_BL)
    orders = jax.vmap(shuffled)(jax.random.split(order_key, N_BL)).astype(jnp.int32)
    at_peak = jnp.take_along_axis(orders, peak_block[:, None], axis=1)
    owner_plan = ((orders - at_peak + heavy_owner) % N_BL).astype(jnp.int32)
    baseline_number = jnp.arange(BASELINE_COUNT, dtype=jnp.int32)
    predictor = baseline_number // BL_DEV
    block_pos = baseline_number % BL_DEV // BLOCK
    lowest = 3 - 4 * predictor // N_BL
    jitter_values = jax.random.randint(jitter_key, (BASELINE_COUNT,), 0, 2)
    exponents = lowest + jnp.where(block_pos == peak_block[predictor], 0, jitter_values)
    return (owner_plan, exponents.astype(jnp.int32))


def draw_owner_plan(key, part):
    return plan_and_exponents(key)[0]


def draw_average_exponent(key, part):
    return plan_and_exponents(key)[1]


def draw_source_group(key, part):
    order = jax.random.permutation(jax.random.fold_in(key, 505), SOURCES)
    return (order // SRC_GRP).astype(jnp.int32)


def touch_ends(array, key, least, largest):
    dims = array.shape
    place = [jax.random.randint(jax.random.fold_in(key, axis), (), 0, dims[axis]) for axis in range(len(dims))]
    array = array.at[tuple(place)].set(least)
    longest = dims.index(max(dims))
    place[longest] = (place[longest] + 1) % dims[longest]
    return array.at[tuple(place)].set(largest)


def block_scale(own_key, shape, shards, smallest, top_value):
    loudness, own = 1.0, jax.random.fold_in(own_key, 6)
    for dim, shards_of in shards:
        draws = jnp.exp(jax.random.uniform(jax.random.fold_in(own, dim), (shards_of,), jnp.float32, smallest / len(shards), top_value / len(shards)))
        loudness = loudness * jnp.repeat(draws, shape[dim] // shards_of).reshape([-1 if axis == dim else 1 for axis in range(len(shape))])
    return loudness


def noise(own_key, dims, width, limit, shards=(), held_as=jnp.bfloat16):
    loudness = block_scale(own_key, dims, shards, -0.22, 0.18) if shards else 1.0
    values = jax.random.normal(own_key, dims, jnp.float32) * width * loudness
    return jnp.minimum(jnp.maximum(values, -limit), limit).astype(held_as)


def setup_inputs(seed: int = 0) -> dict:
    streams_of = jax.random.split(jax.random.key(seed), 12)
    observed = noise(streams_of[0], (F, 2, BDA_ROWS), 1.0, 6.0, ((0, 8), (2, 16)), jnp.float32)
    baseline_uvw_rows = noise(streams_of[1], (3, BASELINE_COUNT * TIME_SAMPLES), 100.0, 600.0, ((1, 16),), jnp.float32)
    frequencies = jnp.clip(jax.random.uniform(streams_of[2], (F,), jnp.float32, 0.8, 1.2), 0.8, 1.2)
    source_offset = jnp.clip(jax.random.uniform(streams_of[3], (2, SOURCES), jnp.float32, -0.05, 0.05), -0.05, 0.05)
    source_flux = jnp.clip(jnp.exp(jax.random.uniform(streams_of[4], (F, SOURCES), jnp.float32, math.log(0.02), math.log(0.3))), 0.02, 0.3)
    source_group = draw_source_group(jax.random.fold_in(streams_of[11], 71), 0)
    direction_gain = noise(streams_of[6], (GROUPS, F, 2, STATION_COUNT), 0.7, 4.2, ((0, 8),), jnp.float32)
    station_first = touch_ends(jax.random.randint(streams_of[7], (BASELINE_COUNT,), 0, STATION_COUNT), jax.random.fold_in(streams_of[7], 1), 0, STATION_COUNT - 1).astype(jnp.int32)
    station_second = touch_ends(jax.random.randint(streams_of[8], (BASELINE_COUNT,), 0, STATION_COUNT), jax.random.fold_in(streams_of[8], 1), 0, STATION_COUNT - 1).astype(jnp.int32)
    average_exponent = draw_average_exponent(jax.random.fold_in(streams_of[11], 71), 0)
    owner_plan = draw_owner_plan(jax.random.fold_in(streams_of[11], 71), 0)
    return {"observed": observed, "baseline_uvw_rows": baseline_uvw_rows, "frequencies": frequencies, "source_offset": source_offset, "source_flux": source_flux, "source_group": source_group, "direction_gain": direction_gain, "station_first": station_first, "station_second": station_second, "average_exponent": average_exponent, "owner_plan": owner_plan}


def layout_tables(average_exponent, owner_plan, owners_total, block_len):
    factor = jnp.left_shift(jnp.ones_like(average_exponent), average_exponent)
    row_count = (TIME_SAMPLES // factor).astype(jnp.int32)
    grouped = row_count.reshape(owners_total, owners_total, block_len)
    block_rows = lax.optimization_barrier(jnp.sum(grouped, axis=2, dtype=jnp.int32))
    in_block = (jnp.cumsum(grouped, axis=2, dtype=jnp.int32) - grouped).reshape(-1)
    owner_ids = jnp.arange(owners_total, dtype=jnp.int32)
    matches = (owner_plan[:, :, None] == owner_ids[None, None, :]).astype(jnp.int32)
    to_owner = lax.optimization_barrier(jnp.sum(block_rows[:, :, None] * matches, axis=1, dtype=jnp.int32))
    before = jnp.cumsum(to_owner, axis=0, dtype=jnp.int32) - to_owner
    offset = jnp.take_along_axis(before, owner_plan, axis=1)
    return (factor, row_count, in_block, offset)

def average_rows(values, exponent, factor):
    leading = values.shape[0]
    shaped = values.reshape(leading, 2, exponent.shape[0], TIME_SAMPLES)
    sample_index = jnp.arange(TIME_SAMPLES, dtype=jnp.int32)
    bin_index = jnp.right_shift(sample_index[:, None], exponent[None, :])
    weights = (bin_index[None, :, :] == sample_index[:, None, None]).astype(jnp.float32) / factor[None, None, :].astype(jnp.float32)
    return jnp.einsum('czbt,itb->czib', shaped, weights, precision=lax.Precision.HIGHEST)

def place_rows(averaged, target, capacity):
    leading = averaged.shape[0]
    flat_values = averaged.reshape(leading, 2, -1)
    empty_rows = jnp.zeros((leading, 2, capacity), jnp.float32)
    return empty_rows.at[:, :, target.reshape(-1)].add(flat_values, mode='drop')

def reference(observed, baseline_uvw_rows, frequencies, source_offset, source_flux, source_group, direction_gain, station_first, station_second, average_exponent, owner_plan):
    member = (source_group[:, None] == jnp.arange(N_DIR, dtype=jnp.int32)[None, :]).astype(jnp.float32)
    east_offset = source_offset[0]
    north_offset = source_offset[1]
    depth_term = jnp.sqrt(1.0 - east_offset * east_offset - north_offset * north_offset) - 1.0
    total_rows = BL_DEV * TIME_SAMPLES
    row_block = min(total_rows, 1024)
    chan_block = 4 if F % 4 == 0 else F
    gain_by_channel = jnp.transpose(direction_gain, (1, 0, 2, 3))
    split_freq = frequencies.reshape(-1, chan_block)
    split_flux = source_flux.reshape(-1, chan_block, source_flux.shape[1])

    def device_rows(pieces):
        coords, first_ids, second_ids = pieces

        def row_piece(coord_block):
            phase_base = 2.0 * jnp.pi * (east_offset[:, None] * coord_block[0][None, :] + north_offset[:, None] * coord_block[1][None, :] + depth_term[:, None] * coord_block[2][None, :])

            def channel_piece(pair_args):
                block_freq, block_flux = pair_args
                angles = block_freq[:, None, None] * phase_base[None, :, :]
                weighted = block_flux[:, :, None] * member[None, :, :]
                real_group = jnp.einsum('ckg,ckr->cgr', weighted, jnp.cos(angles), precision=lax.Precision.HIGHEST)
                imag_group = -jnp.einsum('ckg,ckr->cgr', weighted, jnp.sin(angles), precision=lax.Precision.HIGHEST)
                return (real_group, imag_group)
            real_group, imag_group = lax.map(channel_piece, (split_freq, split_flux))
            return (real_group.reshape(F, N_DIR, row_block), imag_group.reshape(F, N_DIR, row_block))
        blocks = jnp.transpose(coords.reshape(3, -1, row_block), (1, 0, 2))
        real_group, imag_group = lax.map(row_piece, blocks)
        real_group = jnp.transpose(real_group, (1, 2, 0, 3)).reshape(F, N_DIR, total_rows)
        imag_group = jnp.transpose(imag_group, (1, 2, 0, 3)).reshape(F, N_DIR, total_rows)
        gain_first = jnp.take(gain_by_channel, first_ids, axis=3)
        gain_second = jnp.take(gain_by_channel, second_ids, axis=3)
        gain_real = gain_first[:, :, 0] * gain_second[:, :, 0] + gain_first[:, :, 1] * gain_second[:, :, 1]
        gain_imag = gain_first[:, :, 1] * gain_second[:, :, 0] - gain_first[:, :, 0] * gain_second[:, :, 1]
        gain_real = jnp.repeat(gain_real, TIME_SAMPLES, axis=2)
        gain_imag = jnp.repeat(gain_imag, TIME_SAMPLES, axis=2)
        model_real = lax.optimization_barrier(jnp.sum(real_group * gain_real - imag_group * gain_imag, axis=1))
        model_imag = lax.optimization_barrier(jnp.sum(real_group * gain_imag + imag_group * gain_real, axis=1))
        return jnp.stack([model_real, model_imag], axis=1)
    full_model = lax.map(device_rows, (jnp.transpose(baseline_uvw_rows.reshape(3, N_BL, -1), (1, 0, 2)), station_first.reshape(N_BL, -1), station_second.reshape(N_BL, -1)))
    model_rows = jnp.transpose(full_model, (1, 2, 0, 3)).reshape(F, 2, -1)
    block_len = BL_DEV // N_BL
    factor, row_count, in_block, offset = layout_tables(average_exponent, owner_plan, N_BL, block_len)
    averaged = average_rows(model_rows, average_exponent, factor)
    baseline_number = jnp.arange(BL_DEV * N_BL, dtype=jnp.int32)
    predictor = baseline_number // BL_DEV
    block_pos = baseline_number % BL_DEV // block_len
    owner_of = owner_plan[predictor, block_pos]
    row_start = owner_of * CAP_DEV + offset[predictor, block_pos] + in_block
    sample_index = jnp.arange(TIME_SAMPLES, dtype=jnp.int32)
    target = jnp.where(sample_index[:, None] < row_count[None, :], row_start[None, :] + sample_index[:, None], CAP_DEV * N_BL).astype(jnp.int32)
    return observed - place_rows(averaged, target, CAP_DEV * N_BL)
```

```python
import functools

import jax
import jax.numpy as jnp
from jax import lax
from jax.experimental import pallas as pl
from jax.experimental.pallas import tpu as pltpu
from jax.sharding import PartitionSpec as P


TIME = 16
GROUPS = 8
PER_GROUP = 32
CHANNELS = 4
BLOCK_BASELINES = 32
SUB = 16
WINDOW = 384

POLE = 0.2500051432960012
LINE0 = 0.9326632751760481
LINE1 = 0.23550642249107842
SCALE = 2.4653076166502004

VMEM = pl.BlockSpec(memory_space=pltpu.VMEM)
SMEM = pl.BlockSpec(memory_space=pltpu.SMEM)


def split3(values):
    high = values.astype(jnp.bfloat16)
    rest = values - high.astype(jnp.float32)
    middle = rest.astype(jnp.bfloat16)
    low = (rest - middle.astype(jnp.float32)).astype(jnp.bfloat16)
    return high, middle, low


def route_kernel(plan_ref, uvw_ref, out_ref):
    owners = out_ref.shape[0]
    rows = out_ref.shape[2]
    for k in range(owners):
        out_ref[plan_ref[k]] = uvw_ref[:, k * rows : (k + 1) * rows]


def main_kernel(
    offset_ref,
    flux_ref,
    freq_ref,
    total_ref,
    base_ref,
    uvw_ref,
    gain_ref,
    table_ref,
    observed_ref,
    out_ref,
    u_ref,
    wide_ref,
    x_ref,
    model_ref,
    slot_ref,
):
    sources = uvw_ref.shape[0]
    baselines = gain_ref.shape[2]
    stations = gain_ref.shape[2]
    gc = gain_ref.shape[0]
    rows_of = 2 * gc + 16
    lanes = SUB * TIME
    tiles = baselines // (8 * SUB)
    halves = lanes // 128

    for p in range(sources):
        for half in range(2):
            sub = 2 * p + half
            q, s = sub // 8, sub % 8
            for d in range(3):
                u_ref[d, s : s + 1, q * lanes : (q + 1) * lanes] = uvw_ref[
                    p, d : d + 1, half * lanes : (half + 1) * lanes
                ]

    gain_rows = jnp.concatenate([gain_ref[:, 0, :], gain_ref[:, 1, :]], axis=0)
    pieces = jnp.concatenate(split3(gain_rows), axis=0)
    station = lax.broadcasted_iota(jnp.int32, (stations, baselines), 0)

    def picked(row):
        ids = table_ref[row : row + 1, :]
        one_hot = (station == ids).astype(jnp.float32).astype(jnp.bfloat16)
        found = jnp.dot(pieces, one_hot, preferred_element_type=jnp.float32)
        n = 2 * gc
        return found[:n] + found[n : 2 * n] + found[2 * n :]

    first = picked(0)
    second = picked(1)
    pair_real = first[:gc] * second[:gc] + first[gc:] * second[gc:]
    pair_imag = first[gc:] * second[:gc] - first[:gc] * second[gc:]
    starts = table_ref[2:3, :].astype(jnp.float32)
    inverse = table_ref[3:4, :].astype(jnp.float32) * (1.0 / TIME)
    narrow = jnp.concatenate(
        [pair_real, pair_imag, starts, inverse, jnp.zeros((14, baselines), jnp.float32)], axis=0
    )
    narrow = jnp.concatenate(split3(narrow), axis=0)
    per_tile = 8 * SUB
    width = per_tile * TIME
    spread = (
        lax.broadcasted_iota(jnp.int32, (per_tile, width), 0)
        == lax.broadcasted_iota(jnp.int32, (per_tile, width), 1) // TIME
    ).astype(jnp.float32).astype(jnp.bfloat16)
    for q in range(tiles):
        wide = jnp.dot(
            narrow[:, q * per_tile : (q + 1) * per_tile], spread, preferred_element_type=jnp.float32
        )
        wide = wide[:rows_of] + wide[rows_of : 2 * rows_of] + wide[2 * rows_of :]
        for s in range(8):
            for h in range(halves):
                left = s * lanes + h * 128
                wide_ref[h, pl.ds(q * 8 + s, rows_of, stride=8 * tiles), :] = wide[
                    :, left : left + 128
                ]

    model_ref[...] = jnp.zeros_like(model_ref)

    def group(g, carry):
        for k in range(PER_GROUP):
            i = g * PER_GROUP + k
            x_ref[k] = (
                u_ref[0] * offset_ref[0, i]
                + u_ref[1] * offset_ref[1, i]
                + u_ref[2] * offset_ref[2, i]
            )

        def channel(c, carry):
            freq = freq_ref[c]
            a = jnp.zeros((8, tiles * lanes), jnp.float32)
            b = jnp.zeros((8, tiles * lanes), jnp.float32)
            for k in range(PER_GROUP):
                y = x_ref[k] * freq
                t = y - jnp.round(y)
                q = t * t
                tangent = t * (pltpu.reciprocal(POLE - q, approx=True) + (LINE1 * q + LINE0))
                w = flux_ref[c, g * PER_GROUP + k] * pltpu.reciprocal(
                    tangent * tangent + SCALE, approx=True
                )
                a = a + w
                b = b + w * tangent
            cos_sum = (2.0 * SCALE) * a - total_ref[c, g]
            sin_sum = (2.0 * SCALE**0.5) * b
            real_row = (g * CHANNELS + c) * 8 * tiles
            imag_row = real_row + gc * 8 * tiles
            top = pl.multiple_of(c * 16, 16)
            for j in range(halves * tiles):
                q, h = j // halves, j % halves
                gain_real = wide_ref[h, pl.ds(pl.multiple_of(real_row + q * 8, 8), 8), :]
                gain_imag = wide_ref[h, pl.ds(pl.multiple_of(imag_row + q * 8, 8), 8), :]
                cs, sn = cos_sum[:, j * 128 : (j + 1) * 128], sin_sum[:, j * 128 : (j + 1) * 128]
                model_ref[j, pl.ds(top, 8), :] += gain_real * cs + gain_imag * sn
                model_ref[j, pl.ds(top + 8, 8), :] += gain_imag * cs - gain_real * sn
            return carry

        return lax.fori_loop(0, CHANNELS, channel, carry)

    lax.fori_loop(0, GROUPS, group, 0)

    slot_ref[...] = jnp.zeros_like(slot_ref)
    sample = (lax.broadcasted_iota(jnp.int32, (1, lanes), 1) % TIME).astype(jnp.float32)
    slot = lax.broadcasted_iota(jnp.int32, (WINDOW, lanes), 0).astype(jnp.float32)
    start_row = 2 * gc * 8 * tiles
    inverse_row = start_row + 8 * tiles

    def row_of(row):
        return jnp.concatenate([wide_ref[h, row : row + 1, :] for h in range(halves)], axis=1)

    for sub in range(8 * tiles):
        q, s = sub // 8, sub % 8
        base = pl.multiple_of(base_ref[sub], 128)
        inv = row_of(inverse_row + sub)
        target = (
            row_of(start_row + sub)
            + jnp.floor(sample * inv)
            - base.astype(jnp.float32)
        )
        weight = jnp.where(slot == target, inv, 0.0).astype(jnp.bfloat16)
        values = jnp.concatenate(
            [model_ref[q * halves + h, pl.ds(s, 8, stride=8), :] for h in range(halves)], axis=1
        )
        high = values.astype(jnp.bfloat16).astype(jnp.float32)
        both = jnp.concatenate([high, values - high], axis=0).astype(jnp.bfloat16)
        placed = lax.dot_general(
            both, weight, (((1,), (1,)), ((), ())), preferred_element_type=jnp.float32
        )
        slot_ref[:, pl.ds(base, WINDOW)] += placed[:8] + placed[8:]
    capacity = observed_ref.shape[2]
    for c in range(CHANNELS):
        out_ref[c] = observed_ref[c] - slot_ref[2 * c : 2 * c + 2, :capacity]


def on_device(
    observed,
    baseline_uvw_rows,
    frequencies,
    source_offset,
    source_flux,
    source_group,
    direction_gain,
    station_first,
    station_second,
    average_exponent,
    owner_plan,
):
    owners = lax.axis_size("bl")
    me = lax.axis_index("bl")
    my_dir = lax.axis_index("dir")
    local_channels = observed.shape[0]
    capacity = observed.shape[2]
    block_rows = BLOCK_BASELINES * TIME
    f32 = jnp.float32

    gains = lax.all_to_all(direction_gain[0], "dir", 0, 0, tiled=True)

    send = pl.pallas_call(
        route_kernel,
        out_shape=jax.ShapeDtypeStruct((owners, 3, block_rows), f32),
        in_specs=[SMEM, VMEM],
        out_specs=VMEM,
        name="route",
    )(lax.dynamic_index_in_dim(owner_plan, me, 0, keepdims=False), baseline_uvw_rows)
    arrived = lax.all_to_all(send, "bl", 0, 0, tiled=True)

    mine = (owner_plan == me)[:, :, None]
    per_block = (owners, owners, BLOCK_BASELINES)

    def own(ids):
        return jnp.sum(jnp.where(mine, ids.reshape(per_block), 0), axis=1, dtype=jnp.int32).reshape(-1)

    own_first, own_second, own_exponent = own(station_first), own(station_second), own(average_exponent)
    baselines = own_first.shape[0]
    counts = jnp.right_shift(TIME, own_exponent)
    earlier = jnp.arange(baselines)[:, None] < jnp.arange(baselines)[None, :]
    starts = jnp.sum(jnp.where(earlier, counts[:, None], 0), axis=0, dtype=jnp.int32)
    base = (starts.reshape(-1, SUB)[:, 0] // 128) * 128
    table = jnp.stack([own_first, own_second, starts, counts])

    number = jnp.arange(source_group.shape[0])
    before = (source_group[:, None] == source_group[None, :]) & (number[:, None] < number[None, :])
    place = source_group * PER_GROUP + jnp.sum(before, axis=0, dtype=jnp.int32)
    order = place[:, None] == number[None, :]
    own_flux = lax.dynamic_slice_in_dim(source_flux, my_dir * local_channels, local_channels, 0)
    values = jnp.concatenate([source_offset, own_flux], axis=0)
    values = jnp.sum(jnp.where(order[None], values[:, :, None], 0.0), axis=1)
    east, north = values[0], values[1]
    depth = jnp.sqrt(1.0 - east * east - north * north) - 1.0
    offsets = jnp.stack([east, north, depth])
    flux = values[2:]
    total = jnp.sum(flux.reshape(local_channels, GROUPS, PER_GROUP), axis=2)
    own_freq = lax.dynamic_slice_in_dim(frequencies, my_dir * local_channels, local_channels, 0)

    gc = gains.shape[0]
    tiles = baselines // (8 * SUB)
    lanes = SUB * TIME
    return pl.pallas_call(
        main_kernel,
        out_shape=jax.ShapeDtypeStruct(observed.shape, f32),
        in_specs=[SMEM] * 5 + [VMEM] * 4,
        out_specs=VMEM,
        scratch_shapes=[
            pltpu.VMEM((3, 8, tiles * lanes), f32),
            pltpu.VMEM((lanes // 128, (2 * gc + 16) * 8 * tiles, 128), f32),
            pltpu.VMEM((PER_GROUP, 8, tiles * lanes), f32),
            pltpu.VMEM((tiles * lanes // 128, 2 * CHANNELS * 8, 128), f32),
            pltpu.VMEM((2 * CHANNELS, capacity + WINDOW), f32),
        ],
        compiler_params=pltpu.CompilerParams(vmem_limit_bytes=40 << 20),
        name="predict",
    )(offsets, flux, own_freq, total, base, arrived, gains, table, observed)


def solution(mesh):
    in_specs = (
        P("dir", None, "bl"),
        P(None, "bl"),
        P(),
        P(),
        P(),
        P(),
        P("dir", None, None, None),
        P(),
        P(),
        P(),
        P(),
    )
    return jax.shard_map(
        on_device, mesh=mesh, in_specs=in_specs, out_specs=P("dir", None, "bl"), check_vma=False
    )
```

```python
import functools

import jax
import jax.numpy as jnp
from jax import lax
from jax.experimental import pallas as pl
from jax.experimental.pallas import tpu as pltpu
from jax.sharding import PartitionSpec as P


TIME = 16
GROUPS = 8
PER_GROUP = 32
CHANNELS = 4
BLOCK_BASELINES = 32
SUB = 16
WINDOW = 384

POLE = 0.2500051432960012
LINE0 = 0.9326632751760481
LINE1 = 0.23550642249107842
SCALE = 2.4653076166502004

VMEM = pl.BlockSpec(memory_space=pltpu.VMEM)
SMEM = pl.BlockSpec(memory_space=pltpu.SMEM)


def split3(values):
    high = values.astype(jnp.bfloat16)
    rest = values - high.astype(jnp.float32)
    middle = rest.astype(jnp.bfloat16)
    low = (rest - middle.astype(jnp.float32)).astype(jnp.bfloat16)
    return high, middle, low


def route_kernel(plan_ref, uvw_ref, gain_ref, out_ref):
    my_dir, me = lax.axis_index("dir"), lax.axis_index("bl")
    members, _, rows = out_ref.shape
    for k in range(members):
        out_ref[plan_ref[me, k], :3] = uvw_ref[:, k * rows : (k + 1) * rows]
    for j in range(members):
        its_dir = lax.rem(my_dir - me // 2 + j // 2 + GROUPS, GROUPS)
        gains = gain_ref[pl.ds(its_dir * CHANNELS, CHANNELS)]
        out_ref[j, 4:] = jnp.where(me % 2 == 0, gains[:, 0, :], gains[:, 1, :])


def main_kernel(
    offset_ref,
    flux_ref,
    freq_ref,
    total_ref,
    base_ref,
    table_ref,
    observed_ref,
    arrived_ref,
    out_ref,
    u_ref,
    wide_ref,
    x_ref,
    model_ref,
    slot_ref,
    gain_ref,
    narrow_ref,
    staged_ref,
):
    sources, _, stations = arrived_ref.shape
    baselines = table_ref.shape[1]
    gc = GROUPS * CHANNELS
    rows_of = 2 * gc + 8
    lanes = SUB * TIME
    tiles = baselines // (8 * SUB)
    halves = lanes // 128

    for p in range(sources):
        for half in range(2):
            sub = 2 * p + half
            q, s = sub // 8, sub % 8
            for d in range(3):
                u_ref[d, s : s + 1, q * lanes : (q + 1) * lanes] = arrived_ref[
                    p, d : d + 1, half * lanes : (half + 1) * lanes
                ]

    for j in range(GROUPS):
        g = lax.rem(lax.axis_index("dir") - lax.axis_index("bl") // 2 + j + GROUPS, GROUPS)
        gain_ref[pl.ds(pl.multiple_of(g * 8, 8), 8)] = jnp.concatenate(
            [arrived_ref[2 * j, 4:], arrived_ref[2 * j + 1, 4:]], axis=0
        )
    pieces = jnp.concatenate(split3(gain_ref[...]), axis=0)
    station = lax.broadcasted_iota(jnp.int32, (stations, baselines), 0)

    def picked(row):
        ids = table_ref[row : row + 1, :]
        one_hot = jnp.where(station == ids, 1.0, 0.0).astype(jnp.bfloat16)
        found = jnp.dot(pieces, one_hot, preferred_element_type=jnp.float32)
        n = 2 * gc
        return found[:n] + found[n : 2 * n] + found[2 * n :]

    first = picked(0)
    second = picked(1)
    def swapped(rows):
        return pltpu.roll(rows.reshape(GROUPS, 8, baselines), 4, 1).reshape(2 * gc, baselines)

    straight = first * second
    crossed = first * swapped(second)
    part = lax.broadcasted_iota(jnp.int32, (2 * gc, baselines), 0) & CHANNELS
    pair = jnp.where(part == 0, straight + swapped(straight), crossed - swapped(crossed))
    starts = table_ref[2:3, :].astype(jnp.float32)
    inverse = table_ref[3:4, :].astype(jnp.float32) * (1.0 / TIME)
    narrow = jnp.concatenate(
        [pair, starts, inverse, jnp.zeros((6, baselines), jnp.float32)], axis=0
    )
    high = narrow.astype(jnp.bfloat16).astype(jnp.float32)
    narrow_ref[0] = high
    narrow_ref[1] = narrow - high
    per_tile = 8 * SUB
    spread = jnp.where(
        lax.broadcasted_iota(jnp.int32, (per_tile, lanes), 0) & (SUB - 1)
        == lax.shift_right_logical(lax.broadcasted_iota(jnp.int32, (per_tile, lanes), 1), 4),
        1.0,
        0.0,
    ).astype(jnp.bfloat16)
    spread = jnp.concatenate([spread, spread], axis=0)
    in_sublane = jnp.where(
        lax.broadcasted_iota(jnp.int32, (8, per_tile), 0)
        == lax.shift_right_logical(lax.broadcasted_iota(jnp.int32, (8, per_tile), 1), 4),
        1.0,
        0.0,
    )
    for q in range(tiles):
        at = slice(q * per_tile, (q + 1) * per_tile)
        for r in range(rows_of):
            for part in range(2):
                staged_ref[r * 8 : r * 8 + 8, part * per_tile : (part + 1) * per_tile] = (
                    narrow_ref[part, r : r + 1, at] * in_sublane
                )
        wide_ref[q] = jnp.dot(
            staged_ref[...].astype(jnp.bfloat16), spread, preferred_element_type=jnp.float32
        )

    model_ref[...] = jnp.zeros_like(model_ref)

    def group(g, carry):
        for k in range(PER_GROUP):
            i = g * PER_GROUP + k
            x_ref[k] = (
                u_ref[0] * offset_ref[0, i]
                + u_ref[1] * offset_ref[1, i]
                + u_ref[2] * offset_ref[2, i]
            )

        def channel(c, carry):
            freq = freq_ref[c]
            a = jnp.zeros((8, tiles * lanes), jnp.float32)
            b = jnp.zeros((8, tiles * lanes), jnp.float32)
            for k in range(PER_GROUP):
                y = x_ref[k] * freq
                t = y - jnp.round(y)
                q = t * t
                tangent = t * (pltpu.reciprocal(POLE - q, approx=True) + (LINE1 * q + LINE0))
                w = flux_ref[c, g * PER_GROUP + k] * pltpu.reciprocal(
                    tangent * tangent + SCALE, approx=True
                )
                a = a + w
                b = b + w * tangent
            cos_sum = (2.0 * SCALE) * a - total_ref[c, g]
            sin_sum = (2.0 * SCALE**0.5) * b
            real_row = pl.multiple_of((g * 2 * CHANNELS + c) * 8, 8)
            imag_row = pl.multiple_of(real_row + CHANNELS * 8, 8)
            top = pl.multiple_of(c * 16, 16)
            for j in range(halves * tiles):
                q, h = j // halves, j % halves
                lane = slice(h * 128, (h + 1) * 128)
                gain_real = wide_ref[q, pl.ds(real_row, 8), lane]
                gain_imag = wide_ref[q, pl.ds(imag_row, 8), lane]
                cs, sn = cos_sum[:, j * 128 : (j + 1) * 128], sin_sum[:, j * 128 : (j + 1) * 128]
                model_ref[j, pl.ds(top, 8), :] += gain_real * cs + gain_imag * sn
                model_ref[j, pl.ds(top + 8, 8), :] += gain_imag * cs - gain_real * sn
            return carry

        return lax.fori_loop(0, CHANNELS, channel, carry)

    lax.fori_loop(0, GROUPS, group, 0)

    slot_ref[...] = jnp.zeros_like(slot_ref)
    sample = (lax.broadcasted_iota(jnp.int32, (1, lanes), 1) & (TIME - 1)).astype(jnp.float32)
    slot = lax.broadcasted_iota(jnp.int32, (WINDOW, lanes), 0).astype(jnp.float32)
    start_row = 2 * gc * 8
    inverse_row = start_row + 8
    for sub in range(8 * tiles):
        q, s = sub // 8, sub % 8
        base = pl.multiple_of(base_ref[sub], 128)
        inv = wide_ref[q, inverse_row + s : inverse_row + s + 1, :]
        target = (
            wide_ref[q, start_row + s : start_row + s + 1, :]
            + jnp.floor(sample * inv)
            - base.astype(jnp.float32)
        )
        weight = jnp.where(slot == target, inv, 0.0).astype(jnp.bfloat16)
        values = jnp.concatenate(
            [model_ref[q * halves + h, pl.ds(s, 8, stride=8), :] for h in range(halves)], axis=1
        )
        high = values.astype(jnp.bfloat16).astype(jnp.float32)
        both = jnp.concatenate([high, values - high], axis=0).astype(jnp.bfloat16)
        placed = lax.dot_general(
            both, weight, (((1,), (1,)), ((), ())), preferred_element_type=jnp.float32
        )
        slot_ref[:, pl.ds(base, WINDOW)] += placed[:8] + placed[8:]
    capacity = observed_ref.shape[2]
    for c in range(CHANNELS):
        out_ref[c] = observed_ref[c] - slot_ref[2 * c : 2 * c + 2, :capacity]


def on_device(
    observed,
    baseline_uvw_rows,
    frequencies,
    source_offset,
    source_flux,
    source_group,
    direction_gain,
    station_first,
    station_second,
    average_exponent,
    owner_plan,
):
    owners = lax.axis_size("bl")
    me = lax.axis_index("bl")
    my_dir = lax.axis_index("dir")
    local_channels = observed.shape[0]
    capacity = observed.shape[2]
    block_rows = BLOCK_BASELINES * TIME
    f32 = jnp.float32

    send = pl.pallas_call(
        route_kernel,
        out_shape=jax.ShapeDtypeStruct((owners, 8, block_rows), f32),
        in_specs=[SMEM, VMEM, VMEM],
        out_specs=VMEM,
        name="route",
    )(owner_plan, baseline_uvw_rows, direction_gain[0])
    rings = [[(p // 2 + r) % GROUPS * owners + p for p in range(owners)] for r in range(GROUPS)]
    arrived = lax.all_to_all(send, ("dir", "bl"), 0, 0, axis_index_groups=rings, tiled=True)

    mine = (owner_plan == me)[:, :, None]
    per_block = (owners, owners, BLOCK_BASELINES)

    def own(ids):
        held = jnp.sum(jnp.where(mine, ids.reshape(per_block), 0), axis=1, dtype=jnp.int32)
        return held

    own_first, own_second, own_exponent = own(station_first), own(station_second), own(average_exponent)
    baselines = own_first.size
    counts = jnp.right_shift(TIME, own_exponent).reshape(-1)
    earlier = jnp.arange(baselines)[:, None] < jnp.arange(baselines)[None, :]
    starts = jnp.sum(jnp.where(earlier, counts[:, None], 0), axis=0, dtype=jnp.int32)
    held = (own_first, own_second, starts.reshape(owners, -1), counts.reshape(owners, -1))
    table = jnp.stack([h.reshape(-1) for h in held])
    base = (table[2].reshape(-1, SUB)[:, 0] // 128) * 128

    number = jnp.arange(source_group.shape[0])
    before = (source_group[:, None] == source_group[None, :]) & (number[:, None] < number[None, :])
    place = source_group * PER_GROUP + jnp.sum(before, axis=0, dtype=jnp.int32)
    order = place[:, None] == number[None, :]
    own_flux = lax.dynamic_slice_in_dim(source_flux, my_dir * local_channels, local_channels, 0)
    values = jnp.concatenate([source_offset, own_flux], axis=0)
    values = jnp.sum(jnp.where(order[None], values[:, :, None], 0.0), axis=1)
    east, north = values[0], values[1]
    depth = jnp.sqrt(1.0 - east * east - north * north) - 1.0
    offsets = jnp.stack([east, north, depth])
    flux = values[2:]
    total = jnp.sum(flux.reshape(local_channels, GROUPS, PER_GROUP), axis=2)
    own_freq = lax.dynamic_slice_in_dim(frequencies, my_dir * local_channels, local_channels, 0)

    gc = GROUPS * local_channels
    tiles = baselines // (8 * SUB)
    lanes = SUB * TIME
    return pl.pallas_call(
        main_kernel,
        out_shape=jax.ShapeDtypeStruct(observed.shape, f32),
        in_specs=[SMEM] * 5 + [VMEM] * 3,
        out_specs=VMEM,
        scratch_shapes=[
            pltpu.VMEM((3, 8, tiles * lanes), f32),
            pltpu.VMEM((tiles, (2 * gc + 8) * 8, lanes), f32),
            pltpu.VMEM((PER_GROUP, 8, tiles * lanes), f32),
            pltpu.VMEM((tiles * lanes // 128, 2 * CHANNELS * 8, 128), f32),
            pltpu.VMEM((2 * CHANNELS, capacity + WINDOW), f32),
            pltpu.VMEM((2 * gc, direction_gain.shape[3]), f32),
            pltpu.VMEM((2, 2 * gc + 8, baselines), f32),
            pltpu.VMEM(((2 * gc + 8) * 8, 16 * SUB), f32),
        ],
        compiler_params=pltpu.CompilerParams(vmem_limit_bytes=40 << 20),
        name="predict",
    )(offsets, flux, own_freq, total, base, table, observed, arrived)


def solution(mesh):
    in_specs = (
        P("dir", None, "bl"),
        P(None, "bl"),
        P(),
        P(),
        P(),
        P(),
        P("dir", None, None, None),
        P(),
        P(),
        P(),
        P(),
    )
    return jax.shard_map(
        on_device, mesh=mesh, in_specs=in_specs, out_specs=P("dir", None, "bl"), check_vma=False
    )
```

```python
import functools

import jax
import jax.numpy as jnp
from jax import lax
from jax.experimental import pallas as pl
from jax.experimental.pallas import tpu as pltpu
from jax.sharding import PartitionSpec as P


TIME = 16
GROUPS = 8
PER_GROUP = 32
CHANNELS = 4
BLOCK_BASELINES = 32
SUB = 16
WINDOW = 384

POLE = 0.2500051432960012
LINE0 = 0.9326632751760481
LINE1 = 0.23550642249107842
SCALE = 2.4653076166502004

VMEM = pl.BlockSpec(memory_space=pltpu.VMEM)
SMEM = pl.BlockSpec(memory_space=pltpu.SMEM)


def split3(values):
    high = values.astype(jnp.bfloat16)
    rest = values - high.astype(jnp.float32)
    middle = rest.astype(jnp.bfloat16)
    low = (rest - middle.astype(jnp.float32)).astype(jnp.bfloat16)
    return high, middle, low


def route_kernel(plan_ref, uvw_ref, out_ref):
    me = lax.axis_index("bl")
    owners, _, rows = out_ref.shape
    for k in range(owners):
        out_ref[plan_ref[me, k]] = uvw_ref[:, k * rows : (k + 1) * rows]


def sums_kernel(
    offset_ref, flux_ref, freq_ref, total_ref, arrived_ref, sums_ref, u_ref, x_ref
):
    sources, _, rows = arrived_ref.shape
    lanes = SUB * TIME
    width = u_ref.shape[2]

    for p in range(sources):
        for half in range(2):
            sub = 2 * p + half
            q, s = sub // 8, sub % 8
            for d in range(3):
                u_ref[d, s : s + 1, q * lanes : (q + 1) * lanes] = arrived_ref[
                    p, d : d + 1, half * lanes : (half + 1) * lanes
                ]
    def group(g, carry):
        for h in range(2):
            at = slice(h * (width) // 2, (h + 1) * (width) // 2)
            u, v, w = u_ref[0, :, at], u_ref[1, :, at], u_ref[2, :, at]
            for k in range(PER_GROUP):
                i = g * PER_GROUP + k
                x_ref[k, :, at] = u * offset_ref[0, i] + v * offset_ref[1, i] + w * offset_ref[2, i]

        def channel(c, ratio):
            a = jnp.zeros((8, width), jnp.float32)
            b = jnp.zeros((8, width), jnp.float32)
            for k in range(PER_GROUP):
                y = x_ref[k] if ratio is None else x_ref[k] * ratio
                t = y - jnp.round(y)
                q = t * t
                tangent = t * (pltpu.reciprocal(POLE - q, approx=True) + (LINE1 * q + LINE0))
                w = flux_ref[c, g * PER_GROUP + k] * pltpu.reciprocal(
                    tangent * tangent + SCALE, approx=True
                )
                a = a + w
                b = b + w * tangent
            cos_sum = (2.0 * SCALE) * a - total_ref[c, g]
            sin_sum = (2.0 * SCALE**0.5) * b
            sums_ref[0, g * CHANNELS + c] = cos_sum
            sums_ref[1, g * CHANNELS + c] = sin_sum

        channel(0, None)

        def other(c, carry):
            channel(c, freq_ref[c])
            return carry

        return lax.fori_loop(1, CHANNELS, other, carry)

    lax.fori_loop(0, GROUPS, group, 0)


def finish_kernel(
    base_ref,
    table_ref,
    observed_ref,
    sums_ref,
    arrived_ref,
    out_ref,
    wide_ref,
    model_ref,
    slot_ref,
    gain_ref,
    narrow_ref,
    staged_ref,
):
    stations = arrived_ref.shape[2]
    baselines = table_ref.shape[1]
    gc = GROUPS * CHANNELS
    rows_of = 2 * gc + 8
    lanes = SUB * TIME
    tiles = baselines // (8 * SUB)
    halves = lanes // 128

    for g in range(GROUPS):
        part = arrived_ref[g * CHANNELS : (g + 1) * CHANNELS]
        gain_ref[g * 8 : g * 8 + 8] = jnp.concatenate([part[:, 0, :], part[:, 1, :]], axis=0)
    pieces = jnp.concatenate(split3(gain_ref[...]), axis=0)
    station = lax.broadcasted_iota(jnp.int32, (stations, baselines), 0)

    def picked(row):
        ids = table_ref[row : row + 1, :]
        one_hot = jnp.where(station == ids, 1.0, 0.0).astype(jnp.bfloat16)
        found = jnp.dot(pieces, one_hot, preferred_element_type=jnp.float32)
        n = 2 * gc
        return found[:n] + found[n : 2 * n] + found[2 * n :]

    first = picked(0)
    second = picked(1)
    def swapped(rows):
        return pltpu.roll(rows.reshape(GROUPS, 8, baselines), 4, 1).reshape(2 * gc, baselines)

    straight = first * second
    crossed = first * swapped(second)
    part = lax.broadcasted_iota(jnp.int32, (2 * gc, baselines), 0) & CHANNELS
    pair = jnp.where(part == 0, straight + swapped(straight), crossed - swapped(crossed))
    starts = table_ref[2:3, :].astype(jnp.float32)
    inverse = table_ref[3:4, :].astype(jnp.float32) * (1.0 / TIME)
    narrow = jnp.concatenate(
        [pair, starts, inverse, jnp.zeros((6, baselines), jnp.float32)], axis=0
    )
    high = narrow.astype(jnp.bfloat16).astype(jnp.float32)
    narrow_ref[0] = high
    narrow_ref[1] = narrow - high
    per_tile = 8 * SUB
    spread = jnp.where(
        lax.broadcasted_iota(jnp.int32, (per_tile, lanes), 0) & (SUB - 1)
        == lax.shift_right_logical(lax.broadcasted_iota(jnp.int32, (per_tile, lanes), 1), 4),
        1.0,
        0.0,
    ).astype(jnp.bfloat16)
    spread = jnp.concatenate([spread, spread], axis=0)
    in_sublane = jnp.where(
        lax.broadcasted_iota(jnp.int32, (8, per_tile), 0)
        == lax.shift_right_logical(lax.broadcasted_iota(jnp.int32, (8, per_tile), 1), 4),
        1.0,
        0.0,
    )
    for q in range(tiles):
        at = slice(q * per_tile, (q + 1) * per_tile)
        for r in range(rows_of):
            for part in range(2):
                staged_ref[r * 8 : r * 8 + 8, part * per_tile : (part + 1) * per_tile] = (
                    narrow_ref[part, r : r + 1, at] * in_sublane
                )
        wide_ref[q] = jnp.dot(
            staged_ref[...].astype(jnp.bfloat16), spread, preferred_element_type=jnp.float32
        )

    for c in range(CHANNELS):
        for j in range(halves * tiles):
            q, lane = j // halves, slice(j % halves * 128, (j % halves + 1) * 128)
            at = slice(j * 128, (j + 1) * 128)
            real = jnp.zeros((8, 128), jnp.float32)
            imag = jnp.zeros((8, 128), jnp.float32)
            for g in range(GROUPS):
                top = (g * 2 * CHANNELS + c) * 8
                gain_real = wide_ref[q, top : top + 8, lane]
                gain_imag = wide_ref[q, top + 8 * CHANNELS : top + 8 * CHANNELS + 8, lane]
                cs = sums_ref[0, g * CHANNELS + c, :, at]
                sn = sums_ref[1, g * CHANNELS + c, :, at]
                real += gain_real * cs + gain_imag * sn
                imag += gain_imag * cs - gain_real * sn
            model_ref[j, c * 16 : c * 16 + 8, :] = real
            model_ref[j, c * 16 + 8 : c * 16 + 16, :] = imag

    slot_ref[...] = jnp.zeros_like(slot_ref)
    start_row = 2 * gc * 8
    inverse_row = start_row + 8
    sample = (lax.broadcasted_iota(jnp.int32, (8, lanes), 1) & (TIME - 1)).astype(jnp.float32)
    targets = [
        wide_ref[q, start_row : start_row + 8, :]
        + jnp.floor(sample * wide_ref[q, inverse_row : inverse_row + 8, :])
        for q in range(tiles)
    ]
    targets.append(jnp.zeros((128 - 8 * tiles, lanes), jnp.float32))
    target_of = jnp.concatenate(targets, axis=0).T
    slot = lax.broadcasted_iota(jnp.int32, (1, WINDOW), 1)
    for sub in range(8 * tiles):
        q, s = sub // 8, sub % 8
        base = pl.multiple_of(base_ref[sub], 128)
        here = (slot + base).astype(jnp.float32)
        chosen = jnp.where(target_of[:, sub : sub + 1] == here, 1.0, 0.0).astype(jnp.bfloat16)
        values = jnp.concatenate(
            [model_ref[q * halves + h, pl.ds(s, 8, stride=8), :] for h in range(halves)], axis=1
        )
        values = values * wide_ref[q, inverse_row + s : inverse_row + s + 1, :]
        high = values.astype(jnp.bfloat16).astype(jnp.float32)
        both = jnp.concatenate([high, values - high], axis=0).astype(jnp.bfloat16)
        placed = jnp.dot(both, chosen, preferred_element_type=jnp.float32)
        slot_ref[:, pl.ds(base, WINDOW)] += placed[:8] + placed[8:]
    capacity = observed_ref.shape[2]
    for c in range(CHANNELS):
        out_ref[c] = observed_ref[c] - slot_ref[2 * c : 2 * c + 2, :capacity]


def on_device(
    observed,
    baseline_uvw_rows,
    frequencies,
    source_offset,
    source_flux,
    source_group,
    direction_gain,
    station_first,
    station_second,
    average_exponent,
    owner_plan,
):
    owners = lax.axis_size("bl")
    me = lax.axis_index("bl")
    my_dir = lax.axis_index("dir")
    local_channels = observed.shape[0]
    capacity = observed.shape[2]
    block_rows = BLOCK_BASELINES * TIME
    f32 = jnp.float32

    send = pl.pallas_call(
        route_kernel,
        out_shape=jax.ShapeDtypeStruct((owners, 3, block_rows), f32),
        in_specs=[SMEM, VMEM],
        out_specs=VMEM,
        name="route",
    )(owner_plan, baseline_uvw_rows)
    arrived = lax.all_to_all(send, "bl", 0, 0, tiled=True)
    gains = lax.all_to_all(direction_gain[0], "dir", 0, 0, tiled=True)

    mine = (owner_plan == me)[:, :, None]
    per_block = (owners, owners, BLOCK_BASELINES)

    def own(ids):
        held = jnp.sum(jnp.where(mine, ids.reshape(per_block), 0), axis=1, dtype=jnp.int32)
        return held

    own_first, own_second, own_exponent = own(station_first), own(station_second), own(average_exponent)
    baselines = own_first.size
    counts = jnp.right_shift(TIME, own_exponent).reshape(-1)
    earlier = jnp.arange(baselines)[:, None] < jnp.arange(baselines)[None, :]
    starts = jnp.sum(jnp.where(earlier, counts[:, None], 0), axis=0, dtype=jnp.int32)
    held = (own_first, own_second, starts.reshape(owners, -1), counts.reshape(owners, -1))
    table = jnp.stack([h.reshape(-1) for h in held])
    base = (table[2].reshape(-1, SUB)[:, 0] // 128) * 128

    number = jnp.arange(source_group.shape[0])
    before = (source_group[:, None] == source_group[None, :]) & (number[:, None] < number[None, :])
    place = source_group * PER_GROUP + jnp.sum(before, axis=0, dtype=jnp.int32)
    order = place[:, None] == number[None, :]
    own_flux = lax.dynamic_slice_in_dim(source_flux, my_dir * local_channels, local_channels, 0)
    values = jnp.concatenate([source_offset, own_flux], axis=0)
    values = jnp.sum(jnp.where(order[None], values[:, :, None], 0.0), axis=1)
    east, north = values[0], values[1]
    depth = jnp.sqrt(1.0 - east * east - north * north) - 1.0
    flux = values[2:]
    total = jnp.sum(flux.reshape(local_channels, GROUPS, PER_GROUP), axis=2)
    own_freq = lax.dynamic_slice_in_dim(frequencies, my_dir * local_channels, local_channels, 0)
    offsets = jnp.stack([east, north, depth]) * own_freq[0]
    ratios = own_freq / own_freq[0]

    gc = GROUPS * local_channels
    tiles = baselines // (8 * SUB)
    lanes = SUB * TIME
    sums = pl.pallas_call(
        sums_kernel,
        out_shape=jax.ShapeDtypeStruct((2, gc, 8, tiles * lanes), f32),
        in_specs=[SMEM] * 4 + [VMEM],
        out_specs=VMEM,
        scratch_shapes=[
            pltpu.VMEM((3, 8, tiles * lanes), f32),
            pltpu.VMEM((PER_GROUP, 8, tiles * lanes), f32),
        ],
        compiler_params=pltpu.CompilerParams(vmem_limit_bytes=24 << 20),
        cost_estimate=pl.CostEstimate(flops=50 * 10**9, bytes_accessed=10**6, transcendentals=0),
        name="sums",
    )(offsets, flux, ratios, total, arrived)
    return pl.pallas_call(
        finish_kernel,
        out_shape=jax.ShapeDtypeStruct(observed.shape, f32),
        in_specs=[SMEM] + [VMEM] * 4,
        out_specs=VMEM,
        scratch_shapes=[
            pltpu.VMEM((tiles, (2 * gc + 8) * 8, lanes), f32),
            pltpu.VMEM((tiles * lanes // 128, 2 * CHANNELS * 8, 128), f32),
            pltpu.VMEM((2 * CHANNELS, capacity + WINDOW), f32),
            pltpu.VMEM((2 * gc, direction_gain.shape[3]), f32),
            pltpu.VMEM((2, 2 * gc + 8, baselines), f32),
            pltpu.VMEM(((2 * gc + 8) * 8, 16 * SUB), f32),
        ],
        compiler_params=pltpu.CompilerParams(vmem_limit_bytes=24 << 20),
        name="finish",
    )(base, table, observed, sums, gains)


def solution(mesh):
    in_specs = (
        P("dir", None, "bl"),
        P(None, "bl"),
        P(),
        P(),
        P(),
        P(),
        P("dir", None, None, None),
        P(),
        P(),
        P(),
        P(),
    )
    return jax.shard_map(
        on_device, mesh=mesh, in_specs=in_specs, out_specs=P("dir", None, "bl"), check_vma=False
    )
```

```python
import functools

import jax
import jax.numpy as jnp
from jax import lax
from jax.experimental import pallas as pl
from jax.experimental.pallas import tpu as pltpu
from jax.sharding import PartitionSpec as P


TIME = 16
GROUPS = 8
PER_GROUP = 32
CHANNELS = 4
BLOCK_BASELINES = 32
SUB = 16
WINDOW = 384

POLE = 0.2500051432960012
LINE0 = 0.9326632751760481
LINE1 = 0.23550642249107842
SCALE = 2.4653076166502004

VMEM = pl.BlockSpec(memory_space=pltpu.VMEM)
SMEM = pl.BlockSpec(memory_space=pltpu.SMEM)


def split3(values):
    high = values.astype(jnp.bfloat16)
    rest = values - high.astype(jnp.float32)
    middle = rest.astype(jnp.bfloat16)
    low = (rest - middle.astype(jnp.float32)).astype(jnp.bfloat16)
    return high, middle, low


def route_kernel(plan_ref, uvw_ref, out_ref):
    me = lax.axis_index("bl")
    owners, _, rows = out_ref.shape
    for k in range(owners):
        out_ref[plan_ref[me, k]] = uvw_ref[:, k * rows : (k + 1) * rows]


def sums_kernel(
    offset_ref, flux_ref, freq_ref, total_ref, arrived_ref, sums_ref, u_ref, x_ref
):
    sources, _, rows = arrived_ref.shape
    lanes = SUB * TIME
    width = u_ref.shape[2]

    for p in range(sources):
        for half in range(2):
            sub = 2 * p + half
            q, s = sub // 8, sub % 8
            for d in range(3):
                u_ref[d, s : s + 1, q * lanes : (q + 1) * lanes] = arrived_ref[
                    p, d : d + 1, half * lanes : (half + 1) * lanes
                ]
    def group(g, carry):
        for h in range(2):
            at = slice(h * (width) // 2, (h + 1) * (width) // 2)
            u, v, w = u_ref[0, :, at], u_ref[1, :, at], u_ref[2, :, at]
            for k in range(PER_GROUP):
                i = g * PER_GROUP + k
                x_ref[k, :, at] = u * offset_ref[0, i] + v * offset_ref[1, i] + w * offset_ref[2, i]

        def channel(c, ratio):
            a = jnp.zeros((8, width), jnp.float32)
            b = jnp.zeros((8, width), jnp.float32)
            for k in range(PER_GROUP):
                y = x_ref[k] if ratio is None else x_ref[k] * ratio
                t = y - jnp.round(y)
                q = t * t
                tangent = t * (pltpu.reciprocal(POLE - q, approx=True) + (LINE1 * q + LINE0))
                w = flux_ref[c, g * PER_GROUP + k] * pltpu.reciprocal(
                    tangent * tangent + SCALE, approx=True
                )
                a = a + w
                b = b + w * tangent
            cos_sum = (2.0 * SCALE) * a - total_ref[c, g]
            sin_sum = (2.0 * SCALE**0.5) * b
            sums_ref[0, g * CHANNELS + c] = cos_sum
            sums_ref[1, g * CHANNELS + c] = sin_sum

        channel(0, None)
        channel(1, freq_ref[1])

        def other(c, carry):
            channel(c, freq_ref[c])
            return carry

        return lax.fori_loop(2, CHANNELS, other, carry)

    lax.fori_loop(0, GROUPS, group, 0)


def finish_kernel(
    base_ref,
    table_ref,
    observed_ref,
    sums_ref,
    arrived_ref,
    out_ref,
    wide_ref,
    model_ref,
    slot_ref,
    gain_ref,
    narrow_ref,
    staged_ref,
):
    stations = arrived_ref.shape[2]
    baselines = table_ref.shape[1]
    gc = GROUPS * CHANNELS
    rows_of = 2 * gc + 8
    lanes = SUB * TIME
    tiles = baselines // (8 * SUB)
    halves = lanes // 128

    for g in range(GROUPS):
        part = arrived_ref[g * CHANNELS : (g + 1) * CHANNELS]
        gain_ref[g * 8 : g * 8 + 8] = jnp.concatenate([part[:, 0, :], part[:, 1, :]], axis=0)
    pieces = jnp.concatenate(split3(gain_ref[...]), axis=0)
    station = lax.broadcasted_iota(jnp.int32, (stations, baselines), 0)

    def picked(row):
        ids = table_ref[row : row + 1, :]
        one_hot = jnp.where(station == ids, 1.0, 0.0).astype(jnp.bfloat16)
        found = jnp.dot(pieces, one_hot, preferred_element_type=jnp.float32)
        n = 2 * gc
        return found[:n] + found[n : 2 * n] + found[2 * n :]

    first = picked(0)
    second = picked(1)
    def swapped(rows):
        return pltpu.roll(rows.reshape(GROUPS, 8, baselines), 4, 1).reshape(2 * gc, baselines)

    straight = first * second
    crossed = first * swapped(second)
    part = lax.broadcasted_iota(jnp.int32, (2 * gc, baselines), 0) & CHANNELS
    pair = jnp.where(part == 0, straight + swapped(straight), crossed - swapped(crossed))
    starts = table_ref[2:3, :].astype(jnp.float32)
    inverse = table_ref[3:4, :].astype(jnp.float32) * (1.0 / TIME)
    narrow = jnp.concatenate(
        [pair, starts, inverse, jnp.zeros((6, baselines), jnp.float32)], axis=0
    )
    high = narrow.astype(jnp.bfloat16).astype(jnp.float32)
    narrow_ref[0] = high
    narrow_ref[1] = narrow - high
    per_tile = 8 * SUB
    spread = jnp.where(
        lax.broadcasted_iota(jnp.int32, (per_tile, lanes), 0) & (SUB - 1)
        == lax.shift_right_logical(lax.broadcasted_iota(jnp.int32, (per_tile, lanes), 1), 4),
        1.0,
        0.0,
    ).astype(jnp.bfloat16)
    spread = jnp.concatenate([spread, spread], axis=0)
    in_sublane = jnp.where(
        lax.broadcasted_iota(jnp.int32, (8, per_tile), 0)
        == lax.shift_right_logical(lax.broadcasted_iota(jnp.int32, (8, per_tile), 1), 4),
        1.0,
        0.0,
    )
    for q in range(tiles):
        at = slice(q * per_tile, (q + 1) * per_tile)
        for r in range(rows_of):
            for part in range(2):
                staged_ref[r * 8 : r * 8 + 8, part * per_tile : (part + 1) * per_tile] = (
                    narrow_ref[part, r : r + 1, at] * in_sublane
                )
        wide_ref[q] = jnp.dot(
            staged_ref[...].astype(jnp.bfloat16), spread, preferred_element_type=jnp.float32
        )

    for c in range(CHANNELS):
        for j in range(halves * tiles):
            q, lane = j // halves, slice(j % halves * 128, (j % halves + 1) * 128)
            at = slice(j * 128, (j + 1) * 128)
            real = jnp.zeros((8, 128), jnp.float32)
            imag = jnp.zeros((8, 128), jnp.float32)
            for g in range(GROUPS):
                top = (g * 2 * CHANNELS + c) * 8
                gain_real = wide_ref[q, top : top + 8, lane]
                gain_imag = wide_ref[q, top + 8 * CHANNELS : top + 8 * CHANNELS + 8, lane]
                cs = sums_ref[0, g * CHANNELS + c, :, at]
                sn = sums_ref[1, g * CHANNELS + c, :, at]
                real += gain_real * cs + gain_imag * sn
                imag += gain_imag * cs - gain_real * sn
            model_ref[j, c * 16 : c * 16 + 8, :] = real
            model_ref[j, c * 16 + 8 : c * 16 + 16, :] = imag

    slot_ref[...] = jnp.zeros_like(slot_ref)
    start_row = 2 * gc * 8
    inverse_row = start_row + 8
    sample = (lax.broadcasted_iota(jnp.int32, (8, lanes), 1) & (TIME - 1)).astype(jnp.float32)
    targets = [
        wide_ref[q, start_row : start_row + 8, :]
        + jnp.floor(sample * wide_ref[q, inverse_row : inverse_row + 8, :])
        for q in range(tiles)
    ]
    targets.append(jnp.zeros((128 - 8 * tiles, lanes), jnp.float32))
    target_of = jnp.concatenate(targets, axis=0).T
    slot = lax.broadcasted_iota(jnp.int32, (1, WINDOW), 1)
    for sub in range(8 * tiles):
        q, s = sub // 8, sub % 8
        base = pl.multiple_of(base_ref[sub], 128)
        here = (slot + base).astype(jnp.float32)
        chosen = jnp.where(target_of[:, sub : sub + 1] == here, 1.0, 0.0).astype(jnp.bfloat16)
        values = jnp.concatenate(
            [model_ref[q * halves + h, pl.ds(s, 8, stride=8), :] for h in range(halves)], axis=1
        )
        values = values * wide_ref[q, inverse_row + s : inverse_row + s + 1, :]
        high = values.astype(jnp.bfloat16).astype(jnp.float32)
        both = jnp.concatenate([high, values - high], axis=0).astype(jnp.bfloat16)
        placed = jnp.dot(both, chosen, preferred_element_type=jnp.float32)
        slot_ref[:, pl.ds(base, WINDOW)] += placed[:8] + placed[8:]
    capacity = observed_ref.shape[2]
    for c in range(CHANNELS):
        out_ref[c] = observed_ref[c] - slot_ref[2 * c : 2 * c + 2, :capacity]


def on_device(
    observed,
    baseline_uvw_rows,
    frequencies,
    source_offset,
    source_flux,
    source_group,
    direction_gain,
    station_first,
    station_second,
    average_exponent,
    owner_plan,
):
    owners = lax.axis_size("bl")
    me = lax.axis_index("bl")
    my_dir = lax.axis_index("dir")
    local_channels = observed.shape[0]
    capacity = observed.shape[2]
    block_rows = BLOCK_BASELINES * TIME
    f32 = jnp.float32

    send = pl.pallas_call(
        route_kernel,
        out_shape=jax.ShapeDtypeStruct((owners, 3, block_rows), f32),
        in_specs=[SMEM, VMEM],
        out_specs=VMEM,
        name="route",
    )(owner_plan, baseline_uvw_rows)
    arrived = lax.all_to_all(send, "bl", 0, 0, tiled=True)
    gains = lax.all_to_all(direction_gain[0], "dir", 0, 0, tiled=True)

    mine = (owner_plan == me)[:, :, None]
    per_block = (owners, owners, BLOCK_BASELINES)

    def own(ids):
        held = jnp.sum(jnp.where(mine, ids.reshape(per_block), 0), axis=1, dtype=jnp.int32)
        return held

    own_first, own_second, own_exponent = own(station_first), own(station_second), own(average_exponent)
    baselines = own_first.size
    counts = jnp.right_shift(TIME, own_exponent).reshape(-1)
    earlier = jnp.arange(baselines)[:, None] < jnp.arange(baselines)[None, :]
    starts = jnp.sum(jnp.where(earlier, counts[:, None], 0), axis=0, dtype=jnp.int32)
    held = (own_first, own_second, starts.reshape(owners, -1), counts.reshape(owners, -1))
    table = jnp.stack([h.reshape(-1) for h in held])
    base = (table[2].reshape(-1, SUB)[:, 0] // 128) * 128

    number = jnp.arange(source_group.shape[0])
    before = (source_group[:, None] == source_group[None, :]) & (number[:, None] < number[None, :])
    place = source_group * PER_GROUP + jnp.sum(before, axis=0, dtype=jnp.int32)
    order = place[:, None] == number[None, :]
    own_flux = lax.dynamic_slice_in_dim(source_flux, my_dir * local_channels, local_channels, 0)
    values = jnp.concatenate([source_offset, own_flux], axis=0)
    values = jnp.sum(jnp.where(order[None], values[:, :, None], 0.0), axis=1)
    east, north = values[0], values[1]
    depth = jnp.sqrt(1.0 - east * east - north * north) - 1.0
    flux = values[2:]
    total = jnp.sum(flux.reshape(local_channels, GROUPS, PER_GROUP), axis=2)
    own_freq = lax.dynamic_slice_in_dim(frequencies, my_dir * local_channels, local_channels, 0)
    offsets = jnp.stack([east, north, depth]) * own_freq[0]
    ratios = own_freq / own_freq[0]

    gc = GROUPS * local_channels
    tiles = baselines // (8 * SUB)
    lanes = SUB * TIME
    sums = pl.pallas_call(
        sums_kernel,
        out_shape=jax.ShapeDtypeStruct((2, gc, 8, tiles * lanes), f32),
        in_specs=[SMEM] * 4 + [VMEM],
        out_specs=VMEM,
        scratch_shapes=[
            pltpu.VMEM((3, 8, tiles * lanes), f32),
            pltpu.VMEM((PER_GROUP, 8, tiles * lanes), f32),
        ],
        compiler_params=pltpu.CompilerParams(vmem_limit_bytes=24 << 20),
        cost_estimate=pl.CostEstimate(flops=50 * 10**9, bytes_accessed=10**6, transcendentals=0),
        name="sums",
    )(offsets, flux, ratios, total, arrived)
    return pl.pallas_call(
        finish_kernel,
        out_shape=jax.ShapeDtypeStruct(observed.shape, f32),
        in_specs=[SMEM] + [VMEM] * 4,
        out_specs=VMEM,
        scratch_shapes=[
            pltpu.VMEM((tiles, (2 * gc + 8) * 8, lanes), f32),
            pltpu.VMEM((tiles * lanes // 128, 2 * CHANNELS * 8, 128), f32),
            pltpu.VMEM((2 * CHANNELS, capacity + WINDOW), f32),
            pltpu.VMEM((2 * gc, direction_gain.shape[3]), f32),
            pltpu.VMEM((2, 2 * gc + 8, baselines), f32),
            pltpu.VMEM(((2 * gc + 8) * 8, 16 * SUB), f32),
        ],
        compiler_params=pltpu.CompilerParams(vmem_limit_bytes=24 << 20),
        name="finish",
    )(base, table, observed, sums, gains)


def solution(mesh):
    in_specs = (
        P("dir", None, "bl"),
        P(None, "bl"),
        P(),
        P(),
        P(),
        P(),
        P("dir", None, None, None),
        P(),
        P(),
        P(),
        P(),
    )
    return jax.shard_map(
        on_device, mesh=mesh, in_specs=in_specs, out_specs=P("dir", None, "bl"), check_vma=False
    )
```

```python
import functools

import jax
import jax.numpy as jnp
from jax import lax
from jax.experimental import pallas as pl
from jax.experimental.pallas import tpu as pltpu
from jax.sharding import PartitionSpec as P


TIME = 16
GROUPS = 8
PER_GROUP = 32
CHANNELS = 4
BLOCK_BASELINES = 32
SUB = 16
WINDOW = 384

POLE = 0.2500051432960012
LINE0 = 0.9326632751760481
LINE1 = 0.23550642249107842
SCALE = 2.4653076166502004

VMEM = pl.BlockSpec(memory_space=pltpu.VMEM)
SMEM = pl.BlockSpec(memory_space=pltpu.SMEM)


def split3(values):
    high = values.astype(jnp.bfloat16)
    rest = values - high.astype(jnp.float32)
    middle = rest.astype(jnp.bfloat16)
    low = (rest - middle.astype(jnp.float32)).astype(jnp.bfloat16)
    return high, middle, low


def route_kernel(plan_ref, uvw_ref, out_ref):
    me = lax.axis_index("bl")
    owners, _, rows = out_ref.shape
    for k in range(owners):
        out_ref[plan_ref[me, k]] = uvw_ref[:, k * rows : (k + 1) * rows]


def sums_kernel(
    offset_ref, flux_ref, freq_ref, total_ref, arrived_ref, sums_ref, u_ref, x_ref
):
    sources, _, rows = arrived_ref.shape
    lanes = SUB * TIME
    width = u_ref.shape[2]

    for p in range(sources):
        for half in range(2):
            sub = 2 * p + half
            q, s = sub // 8, sub % 8
            for d in range(3):
                u_ref[d, s : s + 1, q * lanes : (q + 1) * lanes] = arrived_ref[
                    p, d : d + 1, half * lanes : (half + 1) * lanes
                ]
    def group(g, carry):
        for h in range(2):
            at = slice(h * (width) // 2, (h + 1) * (width) // 2)
            u, v, w = u_ref[0, :, at], u_ref[1, :, at], u_ref[2, :, at]
            for k in range(PER_GROUP):
                i = g * PER_GROUP + k
                x_ref[k, :, at] = u * offset_ref[0, i] + v * offset_ref[1, i] + w * offset_ref[2, i]

        def channel(c, ratio):
            a = jnp.zeros((8, width), jnp.float32)
            b = jnp.zeros((8, width), jnp.float32)
            for k in range(PER_GROUP):
                y = x_ref[k] if ratio is None else x_ref[k] * ratio
                t = y - jnp.round(y)
                q = t * t
                tangent = t * (pltpu.reciprocal(POLE - q, approx=True) + (LINE1 * q + LINE0))
                w = flux_ref[c, g * PER_GROUP + k] * pltpu.reciprocal(
                    tangent * tangent + SCALE, approx=True
                )
                a = a + w
                b = b + w * tangent
            cos_sum = (2.0 * SCALE) * a - total_ref[c, g]
            sin_sum = (2.0 * SCALE**0.5) * b
            sums_ref[0, g * CHANNELS + c] = cos_sum
            sums_ref[1, g * CHANNELS + c] = sin_sum

        channel(0, None)
        channel(1, freq_ref[1])

        def other(c, carry):
            channel(c, freq_ref[c])
            return carry

        return lax.fori_loop(2, CHANNELS, other, carry)

    lax.fori_loop(0, GROUPS, group, 0)


def finish_kernel(
    base_ref,
    table_ref,
    observed_ref,
    sums_ref,
    arrived_ref,
    out_ref,
    wide_ref,
    model_ref,
    slot_ref,
    gain_ref,
    narrow_ref,
    staged_ref,
):
    stations = arrived_ref.shape[2]
    baselines = table_ref.shape[1]
    gc = GROUPS * CHANNELS
    rows_of = 2 * gc + 8
    lanes = SUB * TIME
    tiles = baselines // (8 * SUB)
    halves = lanes // 128

    for g in range(GROUPS):
        part = arrived_ref[g * CHANNELS : (g + 1) * CHANNELS]
        gain_ref[g * 8 : g * 8 + 8] = jnp.concatenate([part[:, 0, :], part[:, 1, :]], axis=0)
    pieces = jnp.concatenate(split3(gain_ref[...]), axis=0)
    station = lax.broadcasted_iota(jnp.int32, (stations, baselines), 0)

    def picked(row):
        ids = table_ref[row : row + 1, :]
        one_hot = jnp.where(station == ids, 1.0, 0.0).astype(jnp.bfloat16)
        found = jnp.dot(pieces, one_hot, preferred_element_type=jnp.float32)
        n = 2 * gc
        return found[:n] + found[n : 2 * n] + found[2 * n :]

    first = picked(0)
    second = picked(1)
    def swapped(rows):
        return pltpu.roll(rows.reshape(GROUPS, 8, baselines), 4, 1).reshape(2 * gc, baselines)

    straight = first * second
    crossed = first * swapped(second)
    part = lax.broadcasted_iota(jnp.int32, (2 * gc, baselines), 0) & CHANNELS
    pair = jnp.where(part == 0, straight + swapped(straight), crossed - swapped(crossed))
    starts = table_ref[2:3, :].astype(jnp.float32)
    inverse = table_ref[3:4, :].astype(jnp.float32) * (1.0 / TIME)
    narrow = jnp.concatenate(
        [pair, starts, inverse, jnp.zeros((6, baselines), jnp.float32)], axis=0
    )
    high = narrow.astype(jnp.bfloat16).astype(jnp.float32)
    narrow_ref[0] = high
    narrow_ref[1] = narrow - high
    per_tile = 8 * SUB
    spread = jnp.where(
        lax.broadcasted_iota(jnp.int32, (per_tile, lanes), 0) & (SUB - 1)
        == lax.shift_right_logical(lax.broadcasted_iota(jnp.int32, (per_tile, lanes), 1), 4),
        1.0,
        0.0,
    ).astype(jnp.bfloat16)
    spread = jnp.concatenate([spread, spread], axis=0)
    in_sublane = jnp.where(
        lax.broadcasted_iota(jnp.int32, (8, per_tile), 0)
        == lax.shift_right_logical(lax.broadcasted_iota(jnp.int32, (8, per_tile), 1), 4),
        1.0,
        0.0,
    )
    for q in range(tiles):
        at = slice(q * per_tile, (q + 1) * per_tile)
        for r in range(rows_of):
            for part in range(2):
                staged_ref[r * 8 : r * 8 + 8, part * per_tile : (part + 1) * per_tile] = (
                    narrow_ref[part, r : r + 1, at] * in_sublane
                )
        wide_ref[q] = jnp.dot(
            staged_ref[...].astype(jnp.bfloat16), spread, preferred_element_type=jnp.float32
        )

    for c in range(CHANNELS):
        for j in range(halves * tiles):
            q, lane = j // halves, slice(j % halves * 128, (j % halves + 1) * 128)
            at = slice(j * 128, (j + 1) * 128)
            real = jnp.zeros((8, 128), jnp.float32)
            imag = jnp.zeros((8, 128), jnp.float32)
            for g in range(GROUPS):
                top = (g * 2 * CHANNELS + c) * 8
                gain_real = wide_ref[q, top : top + 8, lane]
                gain_imag = wide_ref[q, top + 8 * CHANNELS : top + 8 * CHANNELS + 8, lane]
                cs = sums_ref[0, g * CHANNELS + c, :, at]
                sn = sums_ref[1, g * CHANNELS + c, :, at]
                real += gain_real * cs + gain_imag * sn
                imag += gain_imag * cs - gain_real * sn
            model_ref[j, c * 16 : c * 16 + 8, :] = real
            model_ref[j, c * 16 + 8 : c * 16 + 16, :] = imag

    slot_ref[...] = jnp.zeros_like(slot_ref)
    start_row = 2 * gc * 8
    inverse_row = start_row + 8
    sample = (lax.broadcasted_iota(jnp.int32, (8, lanes), 1) & (TIME - 1)).astype(jnp.float32)
    targets = [
        wide_ref[q, start_row : start_row + 8, :]
        + jnp.floor(sample * wide_ref[q, inverse_row : inverse_row + 8, :])
        for q in range(tiles)
    ]
    targets.append(jnp.zeros((128 - 8 * tiles, lanes), jnp.float32))
    target_of = jnp.concatenate(targets, axis=0).T
    slot = lax.broadcasted_iota(jnp.int32, (1, WINDOW), 1)
    for sub in range(8 * tiles):
        q, s = sub // 8, sub % 8
        base = pl.multiple_of(base_ref[sub], 128)
        here = (slot + base).astype(jnp.float32)
        chosen = jnp.where(target_of[:, sub : sub + 1] == here, 1.0, 0.0).astype(jnp.bfloat16)
        values = jnp.concatenate(
            [model_ref[q * halves + h, pl.ds(s, 8, stride=8), :] for h in range(halves)], axis=1
        )
        values = values * wide_ref[q, inverse_row + s : inverse_row + s + 1, :]
        high = values.astype(jnp.bfloat16).astype(jnp.float32)
        both = jnp.concatenate([high, values - high], axis=0).astype(jnp.bfloat16)
        placed = jnp.dot(both, chosen, preferred_element_type=jnp.float32)
        slot_ref[:, pl.ds(base, WINDOW)] += placed[:8] + placed[8:]
    capacity = observed_ref.shape[2]
    for c in range(CHANNELS):
        out_ref[c] = observed_ref[c] - slot_ref[2 * c : 2 * c + 2, :capacity]


def on_device(
    observed,
    baseline_uvw_rows,
    frequencies,
    source_offset,
    source_flux,
    source_group,
    direction_gain,
    station_first,
    station_second,
    average_exponent,
    owner_plan,
):
    owners = lax.axis_size("bl")
    me = lax.axis_index("bl")
    my_dir = lax.axis_index("dir")
    local_channels = observed.shape[0]
    capacity = observed.shape[2]
    block_rows = BLOCK_BASELINES * TIME
    f32 = jnp.float32

    send = pl.pallas_call(
        route_kernel,
        out_shape=jax.ShapeDtypeStruct((owners, 3, block_rows), f32),
        in_specs=[SMEM, VMEM],
        out_specs=VMEM,
        name="route",
    )(owner_plan, baseline_uvw_rows)
    arrived = lax.all_to_all(send, "bl", 0, 0, tiled=True)
    gains = lax.all_to_all(direction_gain[0], "dir", 0, 0, tiled=True)

    mine = (owner_plan == me)[:, :, None]
    per_block = (owners, owners, BLOCK_BASELINES)

    def own(ids):
        held = jnp.sum(jnp.where(mine, ids.reshape(per_block), 0), axis=1, dtype=jnp.int32)
        return held

    stations = direction_gain.shape[3]
    packed = own((average_exponent * stations + station_first) * stations + station_second)
    own_second = packed % stations
    own_first = packed // stations % stations
    own_exponent = packed // (stations * stations)
    baselines = own_first.size
    counts = jnp.right_shift(TIME, own_exponent).reshape(-1)
    earlier = jnp.arange(baselines)[:, None] < jnp.arange(baselines)[None, :]
    starts = jnp.sum(jnp.where(earlier, counts[:, None], 0), axis=0, dtype=jnp.int32)
    held = (own_first, own_second, starts.reshape(owners, -1), counts.reshape(owners, -1))
    table = jnp.stack([h.reshape(-1) for h in held])
    base = (table[2].reshape(-1, SUB)[:, 0] // 128) * 128

    number = jnp.arange(source_group.shape[0])
    before = (source_group[:, None] == source_group[None, :]) & (number[:, None] < number[None, :])
    place = source_group * PER_GROUP + jnp.sum(before, axis=0, dtype=jnp.int32)
    order = place[:, None] == number[None, :]
    own_flux = lax.dynamic_slice_in_dim(source_flux, my_dir * local_channels, local_channels, 0)
    values = jnp.concatenate([source_offset, own_flux], axis=0)
    values = jnp.sum(jnp.where(order[None], values[:, :, None], 0.0), axis=1)
    east, north = values[0], values[1]
    depth = jnp.sqrt(1.0 - east * east - north * north) - 1.0
    flux = values[2:]
    total = jnp.sum(flux.reshape(local_channels, GROUPS, PER_GROUP), axis=2)
    own_freq = lax.dynamic_slice_in_dim(frequencies, my_dir * local_channels, local_channels, 0)
    offsets = jnp.stack([east, north, depth]) * own_freq[0]
    ratios = own_freq / own_freq[0]

    gc = GROUPS * local_channels
    tiles = baselines // (8 * SUB)
    lanes = SUB * TIME
    sums = pl.pallas_call(
        sums_kernel,
        out_shape=jax.ShapeDtypeStruct((2, gc, 8, tiles * lanes), f32),
        in_specs=[SMEM] * 4 + [VMEM],
        out_specs=VMEM,
        scratch_shapes=[
            pltpu.VMEM((3, 8, tiles * lanes), f32),
            pltpu.VMEM((PER_GROUP, 8, tiles * lanes), f32),
        ],
        compiler_params=pltpu.CompilerParams(vmem_limit_bytes=24 << 20),
        cost_estimate=pl.CostEstimate(flops=50 * 10**9, bytes_accessed=10**6, transcendentals=0),
        name="sums",
    )(offsets, flux, ratios, total, arrived)
    return pl.pallas_call(
        finish_kernel,
        out_shape=jax.ShapeDtypeStruct(observed.shape, f32),
        in_specs=[SMEM] + [VMEM] * 4,
        out_specs=VMEM,
        scratch_shapes=[
            pltpu.VMEM((tiles, (2 * gc + 8) * 8, lanes), f32),
            pltpu.VMEM((tiles * lanes // 128, 2 * CHANNELS * 8, 128), f32),
            pltpu.VMEM((2 * CHANNELS, capacity + WINDOW), f32),
            pltpu.VMEM((2 * gc, direction_gain.shape[3]), f32),
            pltpu.VMEM((2, 2 * gc + 8, baselines), f32),
            pltpu.VMEM(((2 * gc + 8) * 8, 16 * SUB), f32),
        ],
        compiler_params=pltpu.CompilerParams(vmem_limit_bytes=24 << 20),
        name="finish",
    )(base, table, observed, sums, gains)


def solution(mesh):
    in_specs = (
        P("dir", None, "bl"),
        P(None, "bl"),
        P(),
        P(),
        P(),
        P(),
        P("dir", None, None, None),
        P(),
        P(),
        P(),
        P(),
    )
    return jax.shard_map(
        on_device, mesh=mesh, in_specs=in_specs, out_specs=P("dir", None, "bl"), check_vma=False
    )
```
